128 devices in a mesh: dp: 64 (over x, z_lo, y, core), tensor: 2 (over z_hi).
Axes of the slice: x: 4, y: 4, z: 4 (z_hi: 2, z_lo: 2; z = z_hi * 2 + z_lo), core: 2. Of those that a mesh axis runs over, the one named last changes fastest.
Arguments:
- tokens: bfloat16 [64, 512, 768], P('dp'), may hold values from -6 to 6
- counts: int32 [64], P('dp'), may hold values from 216 to 512, as said below
- ln1_gain: bfloat16 [768], replicated, may hold values from 0.5 to 1.5
- ln1_bias: bfloat16 [768], replicated, may hold values from -2 to 2
- qkv_weight: bfloat16 [768, 3, 768], P(None, None, 'tensor'), may hold values from -0.21875 to 0.21875
- qv_bias: bfloat16 [2, 768], P(None, 'tensor'), may hold values from -3 to 3
- out_weight: bfloat16 [768, 768], P('tensor'), may hold values from -3.5 to 3.5
- out_bias: bfloat16 [768], replicated, may hold values from -2 to 2
- ln2_gain: bfloat16 [768], replicated, may hold values from 0.5 to 1.5
- ln2_bias: bfloat16 [768], replicated, may hold values from -2 to 2
- up_weight: bfloat16 [768, 3072], P(None, 'tensor'), may hold values from -0.21875 to 0.21875
- up_bias: bfloat16 [3072], P('tensor'), may hold values from -3 to 3
- down_weight: bfloat16 [3072, 768], P('tensor'), may hold values from -0.21875 to 0.21875
- down_bias: bfloat16 [768], replicated, may hold values from -2 to 2
- cotangent: bfloat16 [64, 512, 768], P('dp'), may hold values from -6 to 6
Outputs:
- block_out: bfloat16 [64, 512, 768], P('dp')
- tokens_grad: bfloat16 [64, 512, 768], P('dp')
- ln1_gain_grad: float32 [768], replicated
- ln1_bias_grad: float32 [768], replicated
- qkv_weight_grad: float32 [768, 3, 768], P(None, None, 'tensor')
- qv_bias_grad: float32 [2, 768], P(None, 'tensor')
- out_weight_grad: float32 [768, 768], P('tensor')
- out_bias_grad: float32 [768], replicated
- ln2_gain_grad: float32 [768], replicated
- ln2_bias_grad: float32 [768], replicated
- up_weight_grad: float32 [768, 3072], P(None, 'tensor')
- up_bias_grad: float32 [3072], P('tensor')
- down_weight_grad: float32 [3072, 768], P('tensor')
- down_bias_grad: float32 [768], replicated
The draws below stay inside these ranges and needn't reach their ends.
Inputs may be any that keep to these rules, and one draw needn't show every extreme that they name: `counts`: each item's real patches: 216, 256 or 512 (crops of 96^3, 64x128x128 and 128^3 voxels); the real patches come first.
All inputs are finite; a program needn't handle non-finite values.
Results may differ from the reference program's by a relative error of at most 0.012.
The reference program's roundings to bfloat16 on the way count: a program that leaves them out, or rounds other values in their place, can miss the bound.
Values sent between devices are 32-bit elements; how exact they have to be, the bound alone decides.
No kernel may reach another device: no remote copies, remote signals or barrier semaphores. Data moves between devices by JAX's collectives and lax.ppermute only.
A program may use at most 128 MiB of HBM per device.

```python
import jax
import jax.numpy as jnp
from jax import lax

D = 768
HEADS = 12
HEAD_DIM = 64
FF = 3072
P_SIZE = 512
ITEMS = 64


def draw_counts(key, part):
    key = jax.random.fold_in(key, 11)
    key_pick, key_full, key_small = jax.random.split(key, 3)
    picks = jax.random.randint(key_pick, (ITEMS,), 0, 3)
    small_len = 27 * P_SIZE // 64
    lengths = jnp.where(picks == 0, small_len, jnp.where(picks == 1, P_SIZE // 2, P_SIZE)).astype(jnp.int32)
    first_slot = jax.random.randint(key_full, (), 0, ITEMS)
    second_slot = (first_slot + 1 + jax.random.randint(key_small, (), 0, ITEMS - 1)) % ITEMS
    lengths = lengths.at[first_slot].set(P_SIZE)
    lengths = lengths.at[second_slot].set(small_len)
    return lengths.astype(jnp.int32)


def block_scale(own_key, extent, shards, least, top_value):
    level = 1.0
    for axis_at, blocks in shards:
        steps = jax.random.uniform(jax.random.fold_in(jax.random.fold_in(own_key, 6), axis_at), (blocks,), jnp.float32, least / len(shards), top_value / len(shards))
        level = level * jnp.repeat(jnp.exp(steps), extent[axis_at] // blocks).reshape((-1,) + (1,) * (len(extent) - 1 - axis_at))
    return level


def noise(key, extent, width, most, cuts=(), held_as=jnp.bfloat16):
    result = width * jax.random.normal(key, extent, jnp.float32)
    if cuts:
        result = result * block_scale(key, extent, cuts, -0.22, 0.18)
    return jnp.clip(result, -most, most).astype(held_as)


def setup_inputs(seed: int = 0) -> dict:
    splits = jax.random.split(jax.random.key(seed), 16)
    tokens = noise(splits[0], (ITEMS, P_SIZE, D), 1.0, 6.0, ((0, 64),))
    counts = draw_counts(jax.random.fold_in(splits[15], 71), 0)
    ln1_gain = jnp.clip(1.0 + 0.1 * jax.random.normal(splits[2], (D,), jnp.float32), 0.5, 1.5).astype(jnp.bfloat16)
    ln1_bias = noise(splits[3], (D,), 0.3, 2.0)
    qkv_weight = noise(splits[4], (D, 3, D), D ** -0.5, 0.21875, ((2, 2),))
    qv_bias = noise(splits[5], (2, D), 0.5, 3.0, ((1, 2),))
    out_weight = noise(splits[6], (D, D), (max(D // 256, 1)) ** -0.5, 3.5, ((0, 2),))
    out_bias = noise(splits[7], (D,), 0.3, 2.0)
    ln2_gain = jnp.clip(1.0 + 0.1 * jax.random.normal(splits[8], (D,), jnp.float32), 0.5, 1.5).astype(jnp.bfloat16)
    ln2_bias = noise(splits[9], (D,), 0.3, 2.0)
    up_weight = noise(splits[10], (D, FF), D ** -0.5, 0.21875, ((1, 2),))
    up_bias = noise(splits[11], (FF,), 0.5, 3.0, ((0, 2),))
    down_weight = noise(splits[12], (FF, D), (FF // 4) ** -0.5, 0.21875, ((0, 2),))
    down_bias = noise(splits[13], (D,), 0.3, 2.0)
    cotangent = noise(splits[14], (ITEMS, P_SIZE, D), 1.0, 6.0, ((0, 64),))
    return {"tokens": tokens, "counts": counts, "ln1_gain": ln1_gain, "ln1_bias": ln1_bias, "qkv_weight": qkv_weight, "qv_bias": qv_bias, "out_weight": out_weight, "out_bias": out_bias, "ln2_gain": ln2_gain, "ln2_bias": ln2_bias, "up_weight": up_weight, "up_bias": up_bias, "down_weight": down_weight, "down_bias": down_bias, "cotangent": cotangent}


@jax.custom_vjp
def low(v):
    return lax.optimization_barrier(v.astype(jnp.bfloat16)).astype(jnp.float32)

@jax.custom_vjp
def low_back(v):
    return v

def low_keep(v):
    return (low(v), None)

def low_pass(kept, grad):
    return (grad,)

def back_keep(v):
    return (v, None)

def back_low(kept, grad):
    return (low(grad),)
low.defvjp(low_keep, low_pass)
low_back.defvjp(back_keep, back_low)
epsilon = 1e-06
highest = lax.Precision.HIGHEST

def matmul(left, right):
    return jnp.dot(left, right, precision=highest)

def layer_norm(value, gain, shift):
    centre = value - lax.optimization_barrier(jnp.mean(value, axis=-1, keepdims=True))
    spread = lax.optimization_barrier(jnp.mean(centre * centre, axis=-1, keepdims=True))
    return centre * lax.rsqrt(spread + epsilon) * gain + shift

def item_forward(params, item, count):
    ln1g, ln1b, wqkv, bqv, wout, bout, ln2g, ln2b, wup, bup, wdown, bdown = params
    score_scale = HEAD_DIM ** (-0.5)
    positions = jnp.arange(P_SIZE, dtype=jnp.int32)
    valid = positions < count
    normed = low(layer_norm(item, ln1g, ln1b))
    packed = matmul(normed, wqkv.reshape(D, 3 * D)).reshape(P_SIZE, 3, D)
    zero_row = jnp.zeros((D,), jnp.float32)
    packed = packed + jnp.stack([bqv[0], zero_row, bqv[1]])
    packed = low(low_back(packed)).reshape(P_SIZE, 3, HEADS, HEAD_DIM)
    query = packed[:, 0]
    key_part = packed[:, 1]
    value_part = packed[:, 2]
    scores = jnp.einsum('qhd,khd->hqk', query, key_part, precision=highest) * score_scale
    scores = jnp.where(valid[None, None, :], scores, -1000000000.0)
    scores = low_back(scores)
    weights = low(jax.nn.softmax(scores, axis=-1))
    attended = jnp.einsum('hqk,khd->qhd', weights, value_part, precision=highest).reshape(P_SIZE, D)
    attended = low(low_back(attended))
    branch = low_back(matmul(attended, wout))
    middle = item + branch + bout
    normed_two = low(layer_norm(middle, ln2g, ln2b))
    upward = low_back(matmul(normed_two, wup) + bup)
    activated = low(jax.nn.gelu(upward, approximate=False))
    downward = low_back(matmul(activated, wdown))
    return (middle + downward + bdown) * valid[:, None].astype(jnp.float32)

def reference(tokens, counts, ln1_gain, ln1_bias, qkv_weight, qv_bias, out_weight, out_bias, ln2_gain, ln2_bias, up_weight, up_bias, down_weight, down_bias, cotangent):
    params = tuple((p.astype(jnp.float32) for p in (ln1_gain, ln1_bias, qkv_weight, qv_bias, out_weight, out_bias, ln2_gain, ln2_bias, up_weight, up_bias, down_weight, down_bias)))
    inputs = tokens.astype(jnp.float32)

    def whole(items, weights_all):

        def one(pair):
            return item_forward(weights_all, pair[0], pair[1])
        return lax.map(jax.checkpoint(one), (items, counts))
    outputs, backward = jax.vjp(whole, inputs, params)
    grad_items, grads = backward(cotangent.astype(jnp.float32))
    g_ln1g, g_ln1b, g_wqkv, g_bqv, g_wout, g_bout, g_ln2g, g_ln2b, g_wup, g_bup, g_wdown, g_bdown = grads
    return (outputs.astype(jnp.bfloat16), grad_items.astype(jnp.bfloat16), g_ln1g, g_ln1b, g_wqkv, g_bqv, g_wout, g_bout, g_ln2g, g_ln2b, g_wup, g_bup, g_wdown, g_bdown)
```

```python
from functools import partial

import jax
import jax.numpy as jnp
import numpy as np
from jax import lax
from jax.sharding import PartitionSpec as P

HEAD_DIM = 64
RING = 4
DP_SHAPE = (4, 2, 4, 2)


epsilon = 1e-06


def dp_moves(move):
    pairs = []
    for source in range(int(np.prod(DP_SHAPE))):
        where = [int(v) for v in np.unravel_index(source, DP_SHAPE)]
        pairs.append((source, int(np.ravel_multi_index(move(*where), DP_SHAPE))))
    return pairs


CORE_SWAP = dp_moves(lambda x, z, y, c: (x, z, y, 1 - c))
Z_SWAP = dp_moves(lambda x, z, y, c: (x, 1 - z, y, c))


def first_shift(k):
    return dp_moves(
        lambda x, z, y, c: ((x + k) % RING, z, y, c) if c == 0 else (x, z, (y + k) % RING, c)
    )


def second_shift(k):
    return dp_moves(
        lambda x, z, y, c: (x, z, (y + k) % RING, c) if c == 0 else ((x + k) % RING, z, y, c)
    )


def places():
    at = lax.axis_index("dp")
    core = at % 2
    y = (at // 2) % RING
    x = at // 16
    return core, jnp.where(core == 0, x, y), jnp.where(core == 0, y, x)


def pick(blocks, at):
    return lax.dynamic_index_in_dim(blocks, at, 0, keepdims=False)


def scatter_ring(blocks, at, shift):
    arrived = [
        lax.ppermute(pick(blocks, (at + k) % RING), "dp", shift(k)) for k in range(1, RING)
    ]
    return pick(blocks, at) + arrived[0] + arrived[1] + arrived[2]


def gather_ring(block, at, shift):
    whole = jnp.zeros((RING,) + block.shape, block.dtype)
    whole = lax.dynamic_update_index_in_dim(whole, block, at, 0)
    for k in range(1, RING):
        arrived = lax.ppermute(block, "dp", shift(k))
        whole = lax.dynamic_update_index_in_dim(whole, arrived, (at - k) % RING, 0)
    return whole


def sum_items(halves):
    core, first, second = places()
    rows, columns = halves.shape[1:]
    mine = pick(halves, core) + lax.ppermute(pick(halves, 1 - core), "dp", CORE_SWAP)
    mine = scatter_ring(mine.reshape(RING, rows // 4, columns), first, first_shift)
    mine = scatter_ring(mine.reshape(RING, rows // 16, columns), second, second_shift)
    mine = mine + lax.ppermute(mine, "dp", Z_SWAP)
    mine = gather_ring(mine, second, second_shift).reshape(rows // 4, columns)
    mine = gather_ring(mine, first, first_shift).reshape(rows, columns)
    other = lax.ppermute(mine, "dp", CORE_SWAP)
    whole = jnp.zeros_like(halves)
    whole = lax.dynamic_update_index_in_dim(whole, mine, core, 0)
    return lax.dynamic_update_index_in_dim(whole, other, 1 - core, 0)


def sum_pair(value):
    return value + lax.ppermute(value, "tensor", [(0, 1), (1, 0)])


def layer_norm(value, gain, shift):
    centre = value - jnp.mean(value, axis=-1, keepdims=True)
    spread = jnp.mean(centre * centre, axis=-1, keepdims=True)
    return centre * lax.rsqrt(spread + epsilon) * gain + shift


def left_trans(left, right):
    return lax.dot_general(
        left, right, (((0,), (0,)), ((), ())), preferred_element_type=jnp.float32
    )


def right_trans(left, right):
    return lax.dot_general(
        left, right, (((1,), (1,)), ((), ())), preferred_element_type=jnp.float32
    )


def attend_item(inputs):
    packed, valid_keys = inputs
    score_scale = HEAD_DIM ** (-0.5)
    query = packed[:, 0]
    key_part = packed[:, 1]
    value_part = packed[:, 2]
    scores = (
        jnp.einsum("qhd,khd->hqk", query, key_part, preferred_element_type=jnp.float32)
        * score_scale
    )
    scores = jnp.where(valid_keys[None, None, :], scores, -1000000000.0)
    largest = jnp.max(scores, axis=-1, keepdims=True)
    expo = jnp.exp(scores - largest)
    total = jnp.sum(expo, axis=-1, keepdims=True)
    probs = expo / total
    log_total = (largest + jnp.log(total))[..., 0]
    attended = jnp.einsum(
        "hqk,khd->qhd", probs.astype(jnp.bfloat16), value_part, preferred_element_type=jnp.float32
    )
    return (attended.astype(jnp.bfloat16), log_total)


def attend_back(inputs):
    packed, valid_keys, log_total, grad_att = inputs
    score_scale = HEAD_DIM ** (-0.5)
    query = packed[:, 0]
    key_part = packed[:, 1]
    value_part = packed[:, 2]
    scores = (
        jnp.einsum("qhd,khd->hqk", query, key_part, preferred_element_type=jnp.float32)
        * score_scale
    )
    scores = jnp.where(valid_keys[None, None, :], scores, -1000000000.0)
    probs = jnp.exp(scores - log_total[..., None])
    grad_value = jnp.einsum(
        "hqk,qhd->khd", probs.astype(jnp.bfloat16), grad_att, preferred_element_type=jnp.float32
    )
    grad_probs = jnp.einsum(
        "qhd,khd->hqk", grad_att, value_part, preferred_element_type=jnp.float32
    )
    grad_scores = probs * (grad_probs - jnp.sum(grad_probs * probs, axis=-1, keepdims=True))
    grad_low = grad_scores.astype(jnp.bfloat16)
    grad_query = (
        jnp.einsum("hqk,khd->qhd", grad_low, key_part, preferred_element_type=jnp.float32)
        * score_scale
    )
    grad_key = (
        jnp.einsum("hqk,qhd->khd", grad_low, query, preferred_element_type=jnp.float32)
        * score_scale
    )
    return jnp.stack([grad_query, grad_key, grad_value], axis=1)


def body(
    tokens,
    counts,
    ln1_gain,
    ln1_bias,
    qkv_weight,
    qv_bias,
    out_weight,
    out_bias,
    ln2_gain,
    ln2_bias,
    up_weight,
    up_bias,
    down_weight,
    down_bias,
    cotangent,
):
    items, patches, width = tokens.shape
    local_width = qkv_weight.shape[2]
    local_heads = local_width // HEAD_DIM
    hidden = up_weight.shape[1]
    rows = items * patches
    positions = jnp.arange(patches, dtype=jnp.int32)
    valid_keys = positions[None, :] < counts[:, None]
    row_valid = valid_keys.astype(jnp.float32).reshape(rows, 1)
    gain_one = ln1_gain.astype(jnp.float32)
    shift_one = ln1_bias.astype(jnp.float32)
    gain_two = ln2_gain.astype(jnp.float32)
    shift_two = ln2_bias.astype(jnp.float32)
    inputs = tokens.astype(jnp.float32).reshape(rows, width)
    normed, norm_one_back = jax.vjp(layer_norm, inputs, gain_one, shift_one)
    normed_low = normed.astype(jnp.bfloat16)
    flat_qkv = qkv_weight.reshape(width, 3 * local_width)
    bias_f = qv_bias.astype(jnp.float32)
    bias_rows = jnp.stack([bias_f[0], jnp.zeros((local_width,), jnp.float32), bias_f[1]])
    packed = (
        jnp.dot(normed_low, flat_qkv, preferred_element_type=jnp.float32).reshape(
            rows, 3, local_width
        )
        + bias_rows
    )
    packed_low = packed.astype(jnp.bfloat16).reshape(items, patches, 3, local_heads, HEAD_DIM)
    attended, log_total = lax.map(attend_item, (packed_low, valid_keys))
    attended_low = attended.reshape(rows, local_width)
    branch = sum_pair(jnp.dot(attended_low, out_weight, preferred_element_type=jnp.float32))
    middle = inputs + branch + out_bias.astype(jnp.float32)
    normed_two, norm_two_back = jax.vjp(layer_norm, middle, gain_two, shift_two)
    normed_two_low = normed_two.astype(jnp.bfloat16)
    upward = jnp.dot(
        normed_two_low, up_weight, preferred_element_type=jnp.float32
    ) + up_bias.astype(jnp.float32)
    activated, gelu_back = jax.vjp(partial(jax.nn.gelu, approximate=False), upward)
    activated_low = activated.astype(jnp.bfloat16)
    grad_out = cotangent.astype(jnp.float32).reshape(rows, width) * row_valid
    down_bias_grad = jnp.sum(grad_out, axis=0)
    grad_down = grad_out.astype(jnp.bfloat16)
    grad_act = right_trans(grad_down, down_weight)
    grad_up = gelu_back(grad_act)[0].astype(jnp.bfloat16)
    grad_normed_two = sum_pair(right_trans(grad_up, up_weight))
    downward = sum_pair(jnp.dot(activated_low, down_weight, preferred_element_type=jnp.float32))
    block_out = ((middle + downward + down_bias.astype(jnp.float32)) * row_valid).astype(
        jnp.bfloat16
    )
    down_weight_grad = left_trans(activated_low, grad_down).reshape(2, hidden // 2, width)
    up_bias_grad = jnp.sum(grad_up.astype(jnp.float32), axis=0)
    up_weight_grad = jnp.stack(
        [
            left_trans(normed_two_low, grad_up[:, : hidden // 2]),
            left_trans(normed_two_low, grad_up[:, hidden // 2 :]),
        ]
    )
    hidden_sums = sum_items(jnp.concatenate([down_weight_grad, up_weight_grad], axis=1))
    grad_mid_norm, ln2_gain_grad, ln2_bias_grad = norm_two_back(grad_normed_two)
    grad_middle = grad_out + grad_mid_norm
    out_bias_grad = jnp.sum(grad_middle, axis=0)
    grad_branch = grad_middle.astype(jnp.bfloat16)
    out_weight_grad = left_trans(attended_low, grad_branch)
    grad_attended = (
        right_trans(grad_branch, out_weight)
        .astype(jnp.bfloat16)
        .reshape(items, patches, local_heads, HEAD_DIM)
    )
    grad_packed = lax.map(attend_back, (packed_low, valid_keys, log_total, grad_attended))
    grad_packed_low = grad_packed.astype(jnp.bfloat16).reshape(rows, 3 * local_width)
    grad_sums_cols = jnp.sum(grad_packed_low.astype(jnp.float32), axis=0).reshape(3, local_width)
    qv_bias_grad = jnp.stack([grad_sums_cols[0], grad_sums_cols[2]])
    qkv_weight_grad = left_trans(normed_low, grad_packed_low)
    grad_normed = sum_pair(right_trans(grad_packed_low, flat_qkv))
    grad_in_norm, ln1_gain_grad, ln1_bias_grad = norm_one_back(grad_normed)
    tokens_grad = (grad_middle + grad_in_norm).astype(jnp.bfloat16).reshape(items, patches, width)

    half = width // 2
    small = jnp.concatenate(
        [
            ln1_gain_grad,
            ln1_bias_grad,
            qv_bias_grad.reshape(-1),
            out_bias_grad,
            ln2_gain_grad,
            ln2_bias_grad,
            up_bias_grad,
            down_bias_grad,
        ]
    )
    small_rows = small.shape[0] // local_width
    small = small.reshape(2, small_rows // 2, local_width)
    spare = (-small.shape[1]) % 128
    qkv_halves = (
        qkv_weight_grad.reshape(2, half, 3, local_width)
        .transpose(0, 2, 1, 3)
        .reshape(2, 3 * half, local_width)
    )
    out_halves = (
        out_weight_grad.reshape(2, local_width // 2, 2, half)
        .transpose(0, 2, 1, 3)
        .reshape(2, local_width, half)
    )
    late_sums = sum_items(
        jnp.concatenate(
            [qkv_halves, out_halves, small, jnp.zeros((2, spare, local_width), jnp.float32)], axis=1
        )
    )
    qkv_end = 3 * half
    out_end = qkv_end + local_width
    qkv_weight_grad = (
        late_sums[:, :qkv_end]
        .reshape(2, 3, half, local_width)
        .transpose(0, 2, 1, 3)
        .reshape(width, 3, local_width)
    )
    out_weight_grad = (
        late_sums[:, qkv_end:out_end]
        .reshape(2, 2, local_width // 2, half)
        .transpose(0, 2, 1, 3)
        .reshape(local_width, width)
    )
    small = late_sums[:, out_end : out_end + small_rows // 2].reshape(-1)
    ends = np.cumsum([width, width, 2 * local_width, width, width, width, hidden, width])
    (
        ln1_gain_grad,
        ln1_bias_grad,
        qv_bias_grad,
        out_bias_grad,
        ln2_gain_grad,
        ln2_bias_grad,
        up_bias_grad,
        down_bias_grad,
    ) = jnp.split(small, ends[:-1])
    down_weight_grad = hidden_sums[:, : hidden // 2].reshape(hidden, width)
    up_weight_grad = jnp.concatenate(
        [hidden_sums[0, hidden // 2 :], hidden_sums[1, hidden // 2 :]], axis=1
    )
    return (
        block_out.reshape(items, patches, width),
        tokens_grad,
        ln1_gain_grad,
        ln1_bias_grad,
        qkv_weight_grad,
        qv_bias_grad.reshape(2, local_width),
        out_weight_grad,
        out_bias_grad,
        ln2_gain_grad,
        ln2_bias_grad,
        up_weight_grad,
        up_bias_grad,
        down_weight_grad,
        down_bias_grad,
    )


def solution(mesh):
    in_specs = (
        P("dp", None, None),
        P("dp"),
        P(),
        P(),
        P(None, None, "tensor"),
        P(None, "tensor"),
        P("tensor", None),
        P(),
        P(),
        P(),
        P(None, "tensor"),
        P("tensor"),
        P("tensor", None),
        P(),
        P("dp", None, None),
    )
    out_specs = (
        P("dp", None, None),
        P("dp", None, None),
        P(),
        P(),
        P(None, None, "tensor"),
        P(None, "tensor"),
        P("tensor", None),
        P(),
        P(),
        P(),
        P(None, "tensor"),
        P("tensor"),
        P("tensor", None),
        P(),
    )
    return jax.shard_map(body, mesh=mesh, in_specs=in_specs, out_specs=out_specs, check_vma=False)
```

```python
from functools import partial

import jax
import jax.numpy as jnp
import numpy as np
from jax import lax
from jax.experimental import pallas as pl
from jax.experimental.pallas import tpu as pltpu
from jax.sharding import PartitionSpec as P

HEAD_DIM = 64
PAIR = 128
RING = 4
DP_SHAPE = (4, 2, 4, 2)
SPLIT = 2
SHARE = 128
TILE = 512
MASKED = -1000000000.0
LOW = jnp.bfloat16
FULL = jnp.float32


epsilon = 1e-06
score_scale = HEAD_DIM ** (-0.5)
root_half = 0.7071067811865476
root_two_pi = 0.3989422804014327


def dp_moves(move):
    pairs = []
    for source in range(int(np.prod(DP_SHAPE))):
        where = [int(v) for v in np.unravel_index(source, DP_SHAPE)]
        pairs.append((source, int(np.ravel_multi_index(move(*where), DP_SHAPE))))
    return pairs


CORE_SWAP = dp_moves(lambda x, z, y, c: (x, z, y, 1 - c))
Z_SWAP = dp_moves(lambda x, z, y, c: (x, 1 - z, y, c))


PLANES = [
    [((x * 2 + z) * RING + y) * 2 + c for c in range(2) for x in range(RING) for y in range(RING)]
    for z in range(2)
]
BOTH_SWAP = [
    (source * 2 + t, target * 2 + 1 - t) for source, target in Z_SWAP for t in range(2)
]


def rings(first):
    groups = []
    for z in range(2):
        for other in range(RING):
            for c in range(2):
                along_x = (c == 0) == first
                group = [(j, other) if along_x else (other, j) for j in range(RING)]
                groups.append([((x * 2 + z) * RING + y) * 2 + c for x, y in group])
    return groups


def first_shift(k):
    return dp_moves(
        lambda x, z, y, c: ((x + k) % RING, z, y, c) if c == 0 else (x, z, (y + k) % RING, c)
    )


def second_shift(k):
    return dp_moves(
        lambda x, z, y, c: (x, z, (y + k) % RING, c) if c == 0 else ((x + k) % RING, z, y, c)
    )


def places():
    at = lax.axis_index("dp")
    return at % 2, at // 16, (at // 2) % RING


class Moves(list):
    def to(self, value, axes, pairs):
        self.append(lax.ppermute(value, axes, pairs))
        return self[-1]

    def over_cores(self, value):
        return self.to(value, "dp", CORE_SWAP)

    def over_tensor(self, value):
        return self.to(value, "tensor", [(0, 1), (1, 0)])

    def around(self, sent, shift):
        return [self.to(s, "dp", shift(k)) for k, s in enumerate(sent, 1)]

    def exchange(self, blocks, groups):
        self.append(lax.all_to_all(blocks, "dp", 0, 0, axis_index_groups=groups))
        return self[-1]


def dot(left, right, left_dim, right_dim):
    return lax.dot_general(
        left, right, (((left_dim,), (right_dim,)), ((), ())), preferred_element_type=FULL
    )


def normalize(value):
    centre = value - jnp.mean(value, axis=-1, keepdims=True)
    scale = lax.rsqrt(jnp.mean(centre * centre, axis=-1, keepdims=True) + epsilon)
    return centre * scale, scale


def norm_back(grad, gain, norm, scale):
    push = grad * gain
    return scale * (
        push
        - jnp.mean(push, axis=-1, keepdims=True)
        - norm * jnp.mean(push * norm, axis=-1, keepdims=True)
    )


def erf(value):
    at = jnp.clip(value, -3.832506856900711, 3.832506856900711)
    square = at * at
    top = jnp.full_like(at, 0.00022905065861350646)
    for c in (
        0.0034082910107109506,
        0.050955695062380861,
        0.18520832239976145,
        1.128379143519084,
    ):
        top = top * square + c
    low = jnp.full_like(at, -1.1791602954361697e-7)
    for c in (
        0.000023547966471313185,
        0.0010179625278914885,
        0.014070470171167667,
        0.11098505178285362,
        0.49746925110067538,
        1.0,
    ):
        low = low * square + c
    return at * top / low


def project_kernel(
    tokens, vectors, weight, normed_t, query_t, key, key_t, value, value_t
):
    norm, _ = normalize(tokens[...].astype(FULL))
    normed = (norm * vectors[0:1, :] + vectors[1:2, :]).astype(LOW)
    normed_t[...] = normed.T
    half = key.shape[1]
    bias = vectors[6:8, :half]
    query_t[...] = ((dot(normed, weight[0], 1, 0) + bias[0:1]).astype(LOW) * score_scale).T
    held = dot(normed, weight[1], 1, 0).astype(LOW)
    key[...] = held
    key_t[...] = held.T
    held = (dot(normed, weight[2], 1, 0) + bias[1:2]).astype(LOW)
    value[...] = held
    value_t[...] = held.T


def attend_kernel(count, query_t, key, value_t, out_weight, attended_t, branch, *weights_t):
    keys, rows = key.shape[0], query_t.shape[1]
    heads = query_t.shape[0] // HEAD_DIM
    valid = lax.broadcasted_iota(jnp.int32, (keys, rows), 0) < count[0]
    for head in range(heads):
        pair = head // 2 * PAIR
        mine = lax.broadcasted_iota(jnp.int32, (PAIR, rows), 0) // HEAD_DIM == head % 2
        query = jnp.where(mine, query_t[pair : pair + PAIR, :], jnp.zeros((), LOW))
        scores = dot(key[:, pair : pair + PAIR], query, 1, 0)
        scores = jnp.where(valid, scores, MASKED)
        expo = jnp.exp(scores - jnp.max(scores, axis=0, keepdims=True))
        total = jnp.sum(expo, axis=0, keepdims=True)
        weights = (expo * (1.0 / total)).astype(LOW)
        weights_t[head][...] = weights
        weights_t[head].done()
        span = slice(head * HEAD_DIM, (head + 1) * HEAD_DIM)
        attended_t[span, :] = dot(value_t[span, :], weights, 1, 0).astype(LOW)
    branch[...] = dot(attended_t[...].T, out_weight[...], 1, 0)


def join_kernel(at, *refs):
    rows = refs[0].shape[0]
    for k, held in enumerate(refs[:RING]):
        owner = lax.rem(at[0] - k + RING, RING)
        refs[RING][pl.ds(pl.multiple_of(owner * rows, 8), rows), :] = held[...]


def clear_kernel(out):
    out[...] = jnp.zeros(out.shape, FULL)


def fold_kernel(blocks, out):
    total = blocks[0]
    for at in range(1, RING):
        total = total + blocks[at]
    out[...] = total


def add_kernel(held, arrived, out):
    out[...] = held[...] + arrived[...]


def quarter_kernel(at, *refs):
    summed, outs = refs[:-RING], refs[-RING:]
    rows = outs[0].shape[0]
    for k in (1, 2, 3, 0):
        owner = lax.rem(at[0] + k, RING)
        span = pl.ds(pl.multiple_of(owner * rows, 8), rows)
        total = summed[0][span, :]
        for held in summed[1:]:
            total = total + held[span, :]
        outs[k][...] = total


def piece_kernel(at, *refs):
    summed, (out, shared) = refs[:-2], refs[-2:]
    total = summed[0][...]
    for held in summed[1:]:
        total = total + held[...]
    out[...] = total
    shared[...] = total[at : at + 8]


def share_kernel(at, holds, mine, arrived, across, both, out):
    out[...] = mine[...] + arrived[...]
    rows = lax.broadcasted_iota(jnp.int32, across.shape, 0)
    extra = jnp.where((rows < 2) & (holds[0] == 1), across[...] + both[...], 0.0)
    out[at : at + 8, :] = out[at : at + 8, :] + extra


def hidden_kernel(
    start,
    count,
    tokens,
    own,
    other,
    vectors,
    up_bias,
    up_weight,
    down_weight,
    cotangent,
    middle,
    normed,
    activated,
    grad_up,
    grad_down,
    grad_normed,
    up_sum,
    down_sum,
    *downward,
):
    hidden = up_weight.shape[1]
    rows, width = middle.shape
    held = tokens[...].astype(FULL) + (own[...] + other[...]) + vectors[4:5, :]
    middle[...] = held
    middle.done()
    norm, _ = normalize(held)
    normed_low = (norm * vectors[2:3, :] + vectors[3:4, :]).astype(LOW)
    normed[...] = normed_low
    normed.done()
    valid = lax.broadcasted_iota(jnp.int32, (rows, 1), 0) + start < count[0]
    grad_out = jnp.where(valid, cotangent[...].astype(FULL), 0.0)
    down_sum[...] = jnp.sum(grad_out, axis=0, keepdims=True)
    grad_low = grad_out.astype(LOW)
    grad_down[...] = grad_low
    grad_down.done()
    for at in range(0, hidden, TILE):
        span = slice(at, at + TILE)
        upward = dot(normed_low, up_weight[:, span], 1, 0) + up_bias[0:1, span]
        share = 0.5 + 0.5 * erf(upward * root_half)
        active = (upward * share).astype(LOW)
        activated[:, span] = active
        slope = share + upward * (root_two_pi * jnp.exp(-0.5 * upward * upward))
        pushed = (dot(grad_low, down_weight[span, :], 1, 1) * slope).astype(LOW)
        grad_up[:, span] = pushed
        up_sum[:, span] = jnp.sum(pushed.astype(FULL), axis=0, keepdims=True)
        back = dot(pushed, up_weight[:, span], 1, 1)
        ahead = dot(active, down_weight[span, :], 1, 0)
        if at == 0:
            grad_normed[...] = back
            total = ahead
        else:
            grad_normed[...] = grad_normed[...] + back
            total = total + ahead
    for at, share in enumerate(downward):
        share[...] = total[at * SHARE : (at + 1) * SHARE]


def attend_back(refs, put):
    (
        grad_down,
        middle,
        own,
        other,
        vectors,
        out_weight,
        query_t,
        key_t,
        value,
        *weights_t,
        grad_branch,
        grad_middle,
        sums,
    ) = refs
    heads = len(weights_t)
    rows = middle.shape[0]
    norm, scale = normalize(middle[...])
    grad = own[...] + other[...]
    sums[0:1, :] = jnp.sum(grad * norm, axis=0, keepdims=True)
    sums[1:2, :] = jnp.sum(grad, axis=0, keepdims=True)
    held = grad_down[...].astype(FULL) + norm_back(grad, vectors[2:3, :], norm, scale)
    grad_middle[...] = held
    grad_middle.done()
    sums[2:3, :] = jnp.sum(held, axis=0, keepdims=True)
    branch = held.astype(LOW)
    grad_branch[...] = branch
    grad_branch.done()
    grad_att = dot(out_weight[...], branch, 1, 1).astype(LOW)
    for head in range(heads):
        pair = head // 2 * PAIR
        span = slice(head * HEAD_DIM, (head + 1) * HEAD_DIM)
        mine = lax.broadcasted_iota(jnp.int32, (PAIR, rows), 0) // HEAD_DIM == head % 2
        grad_own = jnp.where(mine, grad_att[pair : pair + PAIR, :], jnp.zeros((), LOW))
        grad_probs = dot(value[:, pair : pair + PAIR], grad_own, 1, 0)
        weights = weights_t[head][...]
        probs = weights.astype(FULL)
        shift = jnp.sum(grad_probs * probs, axis=0, keepdims=True)
        grad_scores = (probs * (grad_probs - shift)).astype(LOW)
        put(
            span,
            dot(key_t[span, :], grad_scores, 1, 0) * score_scale,
            dot(query_t[span, :], grad_scores, 1, 1),
            dot(grad_att[span, :], weights, 1, 1),
        )


def attend_back_kernel(*refs):
    *refs, grad_query_t, grad_key_t, grad_value_t = refs

    def put(span, query, key, value):
        grad_query_t[span, :] = query
        grad_key_t[span, :] = key
        grad_value_t[span, :] = value

    attend_back(refs, put)


def attend_last_kernel(heads, *refs):
    refs, (queries, keys, values) = refs[:-3], refs[-3:]
    inputs, refs = refs[: 9 + heads], refs[9 + heads :]
    before = [refs[i * (SPLIT - 1) : (i + 1) * (SPLIT - 1)] for i in range(3)]
    refs = refs[3 * (SPLIT - 1) :]
    tokens, weight, grad_branch, grad_middle, back_sums, query, key, value, sums, *shares = refs

    def put(span, grad_query, grad_key, grad_value):
        queries[span, :] = grad_query
        keys[span, :] = sum((k[span, :] for k in before[1]), grad_key)
        values[span, :] = sum((v[span, :] for v in before[2]), grad_value)

    attend_back([*inputs, grad_branch, grad_middle, back_sums], put)
    pieces = [
        jnp.concatenate([q[...] for q in before[0]] + [queries[...]], axis=1),
        keys[...],
        values[...],
    ]
    total = None
    for at, (piece, out) in enumerate(zip(pieces, (query, key, value))):
        low = piece.T.astype(LOW)
        out[...] = low
        out.done()
        if at != 1:
            sums[0:1, (at // 2) * low.shape[1] : (at // 2 + 1) * low.shape[1]] = jnp.sum(
                low.astype(FULL), axis=0, keepdims=True
            )
        term = dot(low, weight[at], 1, 1)
        total = term if total is None else total + term
    for at, share in enumerate(shares):
        share[...] = total[at * SHARE : (at + 1) * SHARE]
        share.done()
    norm, _ = normalize(tokens[...].astype(FULL))
    sums[1:2, :] = jnp.sum(total * norm, axis=0, keepdims=True)
    sums[2:3, :] = jnp.sum(total, axis=0, keepdims=True)


def hidden_grads(owner, refs, put):
    activated, grad_down, normed, grad_up = (refs[i * SPLIT : (i + 1) * SPLIT] for i in range(4))
    tall, short = activated[0].shape[1] // 2, normed[0].shape[1] // 2
    width = grad_down[0].shape[1]
    columns = pl.ds(pl.multiple_of(owner * tall, PAIR), tall)
    active = [a[:, columns].T for a in activated]
    columns = pl.ds(pl.multiple_of(owner * short, PAIR), short)
    inner = [n[:, columns].T for n in normed]
    down_rows, up_rows = tall // 16, short // 16
    rows = down_rows + 2 * up_rows

    def product(lefts, rights, span):
        total = dot(lefts[0][span], rights[0][...], 1, 0)
        for left, right in zip(lefts[1:], rights[1:]):
            total = total + dot(left[span], right[...], 1, 0)
        return total

    for x in range(RING):
        down = product(active, grad_down, slice(x * RING * down_rows, (x + 1) * RING * down_rows))
        up = product(inner, grad_up, slice(x * RING * up_rows, (x + 1) * RING * up_rows))
        for y in range(RING):
            at = pl.multiple_of(jnp.where(owner == 0, x * RING + y, y * RING + x) * rows, 8)
            put(at, down[y * down_rows : (y + 1) * down_rows])
            part = up[y * up_rows : (y + 1) * up_rows]
            put(at + down_rows, part[:, :width])
            put(at + down_rows + up_rows, part[:, width:])


def hidden_away_kernel(away, *refs):
    *refs, lower, upper = refs
    half = lower.shape[0]

    def put(at, value):
        rows = value.shape[0]
        here = pl.ds(pl.multiple_of(jnp.where(at < half, at, at - half), 8), rows)

        @pl.when(at < half)
        def _():
            lower[here, :] = value

        @pl.when(at >= half)
        def _():
            upper[here, :] = value

    hidden_grads(away[0], refs, put)


def hidden_home_kernel(side, *refs):
    *refs, lower, upper, out = refs
    half = lower.shape[0]

    def put(at, value):
        out[pl.ds(pl.multiple_of(at, 8), value.shape[0]), :] = value

    hidden_grads(side[0], refs, put)
    out[:half, :] = out[:half, :] + lower[...]
    out[half:, :] = out[half:, :] + upper[...]


def spread_kernel(gathered, down_out, up_out):
    members, rows, width = gathered.shape
    tall, short = rows // 2, rows // 4
    for at in range(members):
        down_out[at * tall : (at + 1) * tall, :] = gathered[at, :tall, :]
        span = slice(at * short, (at + 1) * short)
        up_out[span, :width] = gathered[at, tall : tall + short, :]
        up_out[span, width:] = gathered[at, tall + short :, :]


def late_grads(at, refs):
    grads, refs = refs[:3], refs[3:]
    attended, branch, back, up_sum, down_sum = (refs[i * SPLIT : (i + 1) * SPLIT] for i in range(5))
    normed_t, sums, out = refs[5 * SPLIT :]
    local, width = attended[0].shape[0], normed_t.shape[0]
    short = width // 2
    mine = pl.ds(pl.multiple_of(at * short, PAIR), short)
    for part, grad in enumerate(grads):
        out[part * short : (part + 1) * short, :] = dot(normed_t[mine, :], grad[...], 1, 0)
    total = dot(attended[0][...].astype(LOW), branch[0][:, mine], 1, 0)
    for a, b in zip(attended[1:], branch[1:]):
        total = total + dot(a[...].astype(LOW), b[:, mine], 1, 0)
    out[3 * short : 3 * short + local, :] = total
    end = 3 * short + local
    out[end:, :] = jnp.zeros((out.shape[0] - end, out.shape[1]), FULL)
    out[end : end + 1, :] = sums[1:2, mine]
    out[end + 1 : end + 2, :] = sums[2:3, mine]
    out[end + 2 : end + 3, :] = sums[0:1, mine]
    for row, of in ((3, 2), (4, 0), (5, 1)):
        out[end + row : end + row + 1, :] = sum(
            (b[of : of + 1, mine] for b in back[1:]), back[0][of : of + 1, mine]
        )
    for part in range(2):
        inner = pl.ds(pl.multiple_of(part * width + at * short, PAIR), short)
        out[end + 6 + part : end + 7 + part, :] = sum(
            (u[:, inner] for u in up_sum[1:]), up_sum[0][:, inner]
        )
    out[end + 8 : end + 9, :] = sum((d[:, mine] for d in down_sum[1:]), down_sum[0][:, mine])
    out.done()


def late_grads_kernel(side, *refs):
    *refs, away, home = refs
    late_grads(1 - side[0], [*refs, away])
    late_grads(side[0], [*refs, home])


def unpack_kernel(side, mine, other, qkv_grad, out_grad, vectors):
    short = out_grad.shape[1] // 2
    local = out_grad.shape[0]
    end = 3 * short + local
    for owner, held in ((side[0], mine), (1 - side[0], other)):
        span = pl.ds(pl.multiple_of(owner * short, PAIR), short)
        for part in range(3):
            qkv_grad[part, span, :] = held[part * short : (part + 1) * short, :]
        out_grad[:, span] = held[3 * short : end, :]
        vectors[:, span] = held[end : end + vectors.shape[0], :]


def finish_kernel(count, tokens, vectors, *refs):
    grad_middle, middle, refs = refs[:SPLIT], refs[SPLIT : 2 * SPLIT], refs[2 * SPLIT :]
    tokens_grad, block_out = refs[-2:]
    count_shares = tokens.shape[0] // SHARE
    each = count_shares // SPLIT
    own, other = refs[: 2 * count_shares], refs[2 * count_shares : -2]
    for at in range(count_shares):
        span = slice(at * SHARE, (at + 1) * SHARE)
        inner = slice(at % each * SHARE, (at % each + 1) * SHARE)
        valid = lax.broadcasted_iota(jnp.int32, (SHARE, 1), 0) + at * SHARE < count[0]
        total = middle[at // each][inner, :] + (own[at][...] + other[at][...]) + vectors[5:6, :]
        block_out[span, :] = jnp.where(valid, total, 0.0).astype(LOW)
    block_out.done()
    for at in range(count_shares):
        span = slice(at * SHARE, (at + 1) * SHARE)
        inner = slice(at % each * SHARE, (at % each + 1) * SHARE)
        norm, scale = normalize(tokens[span, :].astype(FULL))
        grad = own[count_shares + at][...] + other[count_shares + at][...]
        tokens_grad[span, :] = (
            grad_middle[at // each][inner, :] + norm_back(grad, vectors[0:1, :], norm, scale)
        ).astype(LOW)


def far(array):
    return pltpu.with_memory_space_constraint(array, pltpu.HBM)


class Arriving:
    def __init__(self, move, held):
        self.move, self.held = move, held
        self.shape, self.dtype = held.shape, held.dtype

    def __getitem__(self, at):
        if self.move is not None:
            self.move.wait()
            self.move = None
        return self.held[at]


class Leaving:
    def __init__(self, made, result, semaphore):
        self.made, self.result, self.semaphore = made, result, semaphore
        self.shape, self.dtype = made.shape, made.dtype
        self.move = None

    def __getitem__(self, at):
        return self.made[at]

    def __setitem__(self, at, value):
        self.made[at] = value

    def done(self):
        if self.move is None:
            self.move = pltpu.make_async_copy(self.made, self.result, self.semaphore)
            self.move.start()


class Line:
    def __init__(self):
        self.last = []
        self.moves = Moves()

    def pause(self):
        self.call(clear_kernel, [((8, PAIR), FULL)], long=True, near=True, name="pause")

    def call(
        self,
        kernel,
        outs,
        *args,
        scalars=0,
        blocks=None,
        waits=(),
        long=False,
        near=False,
        scratch=(),
        name=None,
    ):
        waits = [*self.last, *waits]
        count, arrays = len(args), args[scalars:]
        seen = [
            (blocks or {}).get(number, (a.shape, (0,) * a.ndim))
            for number, a in enumerate(arrays, scalars)
        ]
        options = dict(
            compiler_params=pltpu.CompilerParams(vmem_limit_bytes=(20 if near else 48) << 20),
            cost_estimate=pl.CostEstimate(
                flops=10**11 if long else 0, bytes_accessed=0, transcendentals=0
            ),
            name=name,
        )
        specs = [pl.BlockSpec(memory_space=pltpu.SMEM)] * scalars
        if near:
            results = pl.pallas_call(
                lambda *refs: kernel(*refs[:count], *refs[count + len(waits) :]),
                grid=(1,),
                out_shape=[jax.ShapeDtypeStruct(*out) for out in outs],
                in_specs=specs
                + [pl.BlockSpec(shape, lambda _, at=at: at) for shape, at in seen]
                + [pl.BlockSpec(memory_space=pl.ANY)] * len(waits),
                out_specs=[
                    pl.BlockSpec(shape, lambda _, n=len(shape): (0,) * n) for shape, _ in outs
                ],
                **options,
            )(*args, *waits)
            self.last = [min(results, key=lambda r: r.size)]
            return list(results)

        moved = [any(a is m for m in self.moves) for a in arrays]

        def run(*refs):
            given, refs = refs[:count], refs[count + len(waits) :]
            results, refs = refs[: len(outs)], refs[len(outs) :]
            held, refs = refs[: len(arrays)], refs[len(arrays) :]
            made, refs = refs[: len(outs)], refs[len(outs) :]
            arrive, leave, *own = refs
            arriving = []
            for at, (array, (shape, spot), into) in enumerate(zip(given[scalars:], seen, held)):
                if shape != array.shape:
                    array = array.at[tuple(pl.ds(i * n, n) for i, n in zip(spot, shape))]
                move = pltpu.make_async_copy(array, into, arrive.at[at])
                move.start()
                arriving.append(Arriving(move, into))
            leaving = [
                Leaving(source, result, leave.at[at])
                for at, (source, result) in enumerate(zip(made, results))
            ]
            kernel(*given[:scalars], *arriving, *leaving, *own)
            for held in arriving:
                if held.move is not None:
                    held.move.wait()
            for out in leaving:
                out.done()
            for out in leaving:
                out.move.wait()

        results = pl.pallas_call(
            run,
            out_shape=[pltpu.HBM(*out) for out in outs],
            in_specs=specs
            + [pl.BlockSpec(memory_space=pl.ANY if m else pltpu.HBM) for m in moved]
            + [pl.BlockSpec(memory_space=pl.ANY)] * len(waits),
            out_specs=[pl.BlockSpec(memory_space=pltpu.HBM)] * len(outs),
            scratch_shapes=[pltpu.VMEM(shape, a.dtype) for a, (shape, _) in zip(arrays, seen)]
            + [pltpu.VMEM(*out) for out in outs]
            + [pltpu.SemaphoreType.DMA((len(arrays),)), pltpu.SemaphoreType.DMA((len(outs),))]
            + [pltpu.VMEM(*own) for own in scratch],
            **options,
        )(*args[:scalars], *(a if m else far(a) for a, m in zip(arrays, moved)), *waits)
        self.last = [min(results, key=lambda r: r.size)]
        return list(results)


def body(
    tokens,
    counts,
    ln1_gain,
    ln1_bias,
    qkv_weight,
    qv_bias,
    out_weight,
    out_bias,
    ln2_gain,
    ln2_bias,
    up_weight,
    up_bias,
    down_weight,
    down_bias,
    cotangent,
):
    items, patches, width = tokens.shape
    local = qkv_weight.shape[2]
    heads = local // HEAD_DIM
    hidden = up_weight.shape[1]
    part = patches // SPLIT
    spot = core, x, y = places()
    side, away = core.reshape(1), (1 - core).reshape(1)
    first, second = jnp.where(core == 0, x, y), jnp.where(core == 0, y, x)
    line = Line()
    moves = line.moves
    tokens = tokens.reshape(patches, width)
    cotangent = cotangent.reshape(patches, width)
    weight = qkv_weight.transpose(1, 0, 2)
    starts = [part * i for i in range(SPLIT)]

    at_row = lax.broadcasted_iota(jnp.int32, (8, width), 0)
    vectors = jnp.zeros((8, width), LOW)
    for row, vector in enumerate((ln1_gain, ln1_bias, ln2_gain, ln2_bias, out_bias, down_bias)):
        vectors = jnp.where(at_row == row, vector[None, :], vectors)
    for row in range(2):
        both = jnp.concatenate([qv_bias[row], qv_bias[row]])
        vectors = jnp.where(at_row == 6 + row, both[None, :], vectors)
    vectors = vectors.astype(FULL)
    up_bias = jnp.broadcast_to(up_bias.astype(FULL)[None, :], (8, hidden))

    normed_t, query_t, key, key_t, value, value_t = line.call(
        project_kernel,
        [((width, patches), LOW)]
        + [((local, patches), LOW), ((patches, local), LOW)]
        + [((local, patches), LOW), ((patches, local), LOW), ((local, patches), LOW)],
        tokens,
        vectors,
        weight,
        name="project",
    )

    def attend(at):
        attended, branch, *weights = line.call(
            attend_kernel,
            [((local, part), LOW), ((part, width), FULL)] + [((patches, part), LOW)] * heads,
            counts,
            query_t,
            key,
            value_t,
            out_weight,
            scalars=1,
            blocks={1: ((local, part), (0, at))},
            name="attend",
        )
        return attended, branch, weights

    attended, branches, weights = zip(*[attend(at) for at in range(SPLIT)])
    others = [moves.over_tensor(b) for b in branches]

    def feed_forward(at):
        block = ((part, width), (at, 0))
        return line.call(
            partial(hidden_kernel, starts[at]),
            [
                ((part, width), FULL),
                ((part, width), LOW),
                ((part, hidden), LOW),
                ((part, hidden), LOW),
                ((part, width), LOW),
                ((part, width), FULL),
                ((1, hidden), FULL),
                ((1, width), FULL),
            ]
            + [((SHARE, width), FULL)] * (part // SHARE),
            counts,
            tokens,
            branches[at],
            others[at],
            vectors,
            up_bias,
            up_weight,
            down_weight,
            cotangent,
            scalars=1,
            blocks={1: block, 8: block},
            name="hidden",
        )

    (
        middle,
        normed_two,
        activated,
        grad_up,
        grad_down,
        grad_normed_two,
        up_sum,
        down_sum,
        *downward,
    ) = zip(*[feed_forward(at) for at in range(SPLIT)])
    grad_others = [moves.over_tensor(g) for g in grad_normed_two]

    grads_in = [*activated, *grad_down, *normed_two, *grad_up]
    block_rows = hidden // 32 + width // 16
    hidden_away = line.call(
        hidden_away_kernel,
        [((8 * block_rows, width), FULL)] * 2,
        away,
        *grads_in,
        scalars=1,
        name="hidden_away",
    )
    hidden_arrived = [moves.over_cores(a) for a in hidden_away]

    def back_in(at):
        return [
            grad_down[at],
            middle[at],
            grad_normed_two[at],
            grad_others[at],
            vectors,
            out_weight,
            query_t,
            key_t,
            value,
            *weights[at],
        ]

    back_out = [((part, width), LOW), ((part, width), FULL), ((8, width), FULL)]
    back_held = [((local, part), FULL), ((local, patches), FULL), ((local, patches), FULL)]
    back_parts = [
        line.call(
            attend_back_kernel,
            back_out + back_held,
            *back_in(at),
            blocks={6: ((local, part), (0, at))},
            long=True,
            name="attend_back",
        )
        for at in range(SPLIT - 1)
    ]
    hidden_mine = line.call(
        hidden_home_kernel,
        [((16 * block_rows, width), FULL)],
        side,
        *grads_in,
        *hidden_arrived,
        scalars=1,
        name="hidden_home",
    )[0]
    hidden_mine = moves.exchange(hidden_mine.reshape(RING, 4 * block_rows, width), rings(True))
    grad_branch, grad_middle, back_sums, grad_query, grad_key, grad_value = zip(*back_parts)
    branch_last, middle_last, sums_last, grad_query, grad_key, grad_value, late, *shares = line.call(
        partial(attend_last_kernel, heads),
        back_out
        + [((patches, local), LOW)] * 3
        + [((8, width), FULL)]
        + [((SHARE, width), FULL)] * (patches // SHARE),
        *back_in(SPLIT - 1),
        *grad_query,
        *grad_key,
        *grad_value,
        tokens,
        weight,
        blocks={6: ((local, part), (0, SPLIT - 1))},
        scratch=back_held,
        long=True,
        name="attend_last",
    )
    grad_branch += (branch_last,)
    grad_middle += (middle_last,)
    back_sums += (sums_last,)
    late_rows = 3 * width // 2 + local + 128

    shares = [*(d[at] for at in range(SPLIT) for d in downward), *shares]
    other_shares = [moves.over_tensor(s) for s in shares]
    late_away, late_home = line.call(
        late_grads_kernel,
        [((late_rows, local), FULL)] * 2,
        side,
        grad_query,
        grad_key,
        grad_value,
        *attended,
        *grad_branch,
        *back_sums,
        *up_sum,
        *down_sum,
        normed_t,
        late,
        scalars=1,
        name="late_grads",
    )
    late_arrived = moves.over_cores(late_away)

    def fold(blocks, *waits, near=False):
        return line.call(
            fold_kernel,
            [(blocks.shape[1:], FULL)],
            blocks,
            waits=waits,
            near=near,
            name="hidden_sums",
        )[0]

    def quarter(summed, at, *waits, near=True):
        rows = summed[0].shape[0] // RING
        return line.call(
            quarter_kernel,
            [((rows, local), FULL)] * RING,
            at.reshape(1),
            *summed,
            scalars=1,
            waits=waits,
            near=near,
            name="late_sums",
        )

    def join(block, arrived, at, *waits):
        return line.call(
            join_kernel,
            [((RING * block.shape[0], local), FULL)],
            at.reshape(1),
            block,
            *arrived,
            scalars=1,
            waits=waits,
            near=True,
            name="late_join",
        )[0]

    hidden_mine = fold(hidden_mine, other_shares[0])
    hidden_mine = moves.exchange(hidden_mine.reshape(RING, block_rows, width), rings(False))
    mine, *sent = quarter([late_home, late_arrived], first, near=False)
    late_sums = [mine, *moves.around(sent, first_shift)]
    line.pause()
    hidden_mine = fold(hidden_mine, near=True)
    hidden_arrived = moves.to(hidden_mine, "dp", Z_SWAP)
    mine, *sent = quarter(late_sums, second, *other_shares[1:3])
    late_sums = [mine, *moves.around(sent, second_shift)]
    hidden_mine = line.call(
        add_kernel,
        [(hidden_mine.shape, FULL)],
        hidden_mine,
        hidden_arrived,
        near=True,
        name="hidden_sums",
    )[0]
    hidden_all = lax.all_gather(
        hidden_mine, "dp", axis_index_groups=PLANES, axis=0, tiled=False
    )
    norm_block, norm_at = divmod(3 * width // 2 + local, late_rows // 16)
    mine, shared = line.call(
        partial(piece_kernel, norm_at),
        [(mine.shape, FULL), ((8, local), FULL)],
        *late_sums,
        waits=[other_shares[3]],
        near=True,
        name="late_piece",
    )
    arrived = [
        moves.to(mine, "dp", Z_SWAP),
        moves.over_tensor(shared),
        moves.to(shared, ("dp", "tensor"), BOTH_SWAP),
    ]
    mine = line.call(
        partial(share_kernel, norm_at),
        [(mine.shape, FULL)],
        (first * RING + second == norm_block).astype(jnp.int32).reshape(1),
        mine,
        *arrived,
        scalars=1,
        near=True,
        name="late_share",
    )[0]
    arrived = moves.around([mine] * (RING - 1), second_shift)
    mine = join(mine, arrived, second, other_shares[4])
    arrived = moves.around([mine] * (RING - 1), first_shift)
    mine = join(mine, arrived, first, *other_shares[5:7])
    other = moves.over_cores(mine)
    tokens_grad, block_out = line.call(
        finish_kernel,
        [((patches, width), LOW)] * 2,
        counts,
        tokens,
        vectors,
        *grad_middle,
        *middle,
        *shares,
        *other_shares,
        scalars=1,
        name="finish",
    )
    qkv_weight_grad, out_weight_grad, small = line.call(
        unpack_kernel,
        [((3, width, local), FULL), ((local, width), FULL), ((9, width), FULL)],
        side,
        mine,
        other,
        scalars=1,
        name="unpack",
    )
    each = 8
    members = 32 // each
    down_weight_grad, up_weight_grad = pl.pallas_call(
        lambda gathered, _, *outs: spread_kernel(gathered, *outs),
        grid=(each,),
        out_shape=[
            jax.ShapeDtypeStruct((hidden, width), FULL),
            jax.ShapeDtypeStruct((width, hidden), FULL),
        ],
        in_specs=[
            pl.BlockSpec((members, *hidden_all.shape[1:]), lambda i: (i, 0, 0)),
            pl.BlockSpec(memory_space=pl.ANY),
        ],
        out_specs=[
            pl.BlockSpec((hidden // each, width), lambda i: (i, 0)),
            pl.BlockSpec((width // each, hidden), lambda i: (i, 0)),
        ],
        compiler_params=pltpu.CompilerParams(vmem_limit_bytes=48 << 20),
        name="spread",
    )(hidden_all, *line.last)
    line.last = [down_weight_grad]
    qkv_weight_grad = qkv_weight_grad.transpose(1, 0, 2)
    ln1_gain_grad, ln1_bias_grad, qv_bias_grad, out_bias_grad, ln2_gain_grad, ln2_bias_grad = (
        small[i] for i in range(6)
    )
    up_bias_grad = small[6:8].reshape(hidden)
    down_bias_grad = small[8]
    return (
        block_out.reshape(items, patches, width),
        tokens_grad.reshape(items, patches, width),
        ln1_gain_grad,
        ln1_bias_grad,
        qkv_weight_grad,
        qv_bias_grad.reshape(2, local),
        out_weight_grad,
        out_bias_grad,
        ln2_gain_grad,
        ln2_bias_grad,
        up_weight_grad,
        up_bias_grad,
        down_weight_grad,
        down_bias_grad,
    )


def solution(mesh):
    in_specs = (
        P("dp", None, None),
        P("dp"),
        P(),
        P(),
        P(None, None, "tensor"),
        P(None, "tensor"),
        P("tensor", None),
        P(),
        P(),
        P(),
        P(None, "tensor"),
        P("tensor"),
        P("tensor", None),
        P(),
        P("dp", None, None),
    )
    out_specs = (
        P("dp", None, None),
        P("dp", None, None),
        P(),
        P(),
        P(None, None, "tensor"),
        P(None, "tensor"),
        P("tensor", None),
        P(),
        P(),
        P(),
        P(None, "tensor"),
        P("tensor"),
        P("tensor", None),
        P(),
    )
    return jax.shard_map(body, mesh=mesh, in_specs=in_specs, out_specs=out_specs, check_vma=False)
```

```python
from functools import partial

import jax
import jax.numpy as jnp
import numpy as np
from jax import lax
from jax.experimental import pallas as pl
from jax.experimental.pallas import tpu as pltpu
from jax.sharding import PartitionSpec as P

HEAD_DIM = 64
PAIR = 128
RING = 4
DP_SHAPE = (4, 2, 4, 2)
SPLIT = 2
SHARE = 128
TILE = 512
MASKED = -1000000000.0
LOW = jnp.bfloat16
FULL = jnp.float32


epsilon = 1e-06
score_scale = HEAD_DIM ** (-0.5)
root_half = 0.7071067811865476
root_two_pi = 0.3989422804014327


def dp_moves(move):
    pairs = []
    for source in range(int(np.prod(DP_SHAPE))):
        where = [int(v) for v in np.unravel_index(source, DP_SHAPE)]
        pairs.append((source, int(np.ravel_multi_index(move(*where), DP_SHAPE))))
    return pairs


CORE_SWAP = dp_moves(lambda x, z, y, c: (x, z, y, 1 - c))
Z_SWAP = dp_moves(lambda x, z, y, c: (x, 1 - z, y, c))


PLANES = [
    [((x * 2 + z) * RING + y) * 2 + c for c in range(2) for x in range(RING) for y in range(RING)]
    for z in range(2)
]
BOTH_SWAP = [
    (source * 2 + t, target * 2 + 1 - t) for source, target in Z_SWAP for t in range(2)
]


def rings(first):
    groups = []
    for z in range(2):
        for other in range(RING):
            for c in range(2):
                along_x = (c == 0) == first
                group = [(j, other) if along_x else (other, j) for j in range(RING)]
                groups.append([((x * 2 + z) * RING + y) * 2 + c for x, y in group])
    return groups


def first_shift(k):
    return dp_moves(
        lambda x, z, y, c: ((x + k) % RING, z, y, c) if c == 0 else (x, z, (y + k) % RING, c)
    )


def second_shift(k):
    return dp_moves(
        lambda x, z, y, c: (x, z, (y + k) % RING, c) if c == 0 else ((x + k) % RING, z, y, c)
    )


def places():
    at = lax.axis_index("dp")
    return at % 2, at // 16, (at // 2) % RING


class Moves(list):
    def to(self, value, axes, pairs):
        self.append(lax.ppermute(value, axes, pairs))
        return self[-1]

    def over_cores(self, value):
        return self.to(value, "dp", CORE_SWAP)

    def over_tensor(self, value):
        return self.to(value, "tensor", [(0, 1), (1, 0)])

    def around(self, sent, shift):
        return [self.to(s, "dp", shift(k)) for k, s in enumerate(sent, 1)]

    def exchange(self, blocks, groups):
        self.append(lax.all_to_all(blocks, "dp", 0, 0, axis_index_groups=groups))
        return self[-1]


def dot(left, right, left_dim, right_dim):
    return lax.dot_general(
        left, right, (((left_dim,), (right_dim,)), ((), ())), preferred_element_type=FULL
    )


def normalize(value):
    centre = value - jnp.mean(value, axis=-1, keepdims=True)
    scale = lax.rsqrt(jnp.mean(centre * centre, axis=-1, keepdims=True) + epsilon)
    return centre * scale, scale


def norm_back(grad, gain, norm, scale):
    push = grad * gain
    return scale * (
        push
        - jnp.mean(push, axis=-1, keepdims=True)
        - norm * jnp.mean(push * norm, axis=-1, keepdims=True)
    )


def erf(value):
    at = jnp.clip(value, -3.832506856900711, 3.832506856900711)
    square = at * at
    top = jnp.full_like(at, 0.00022905065861350646)
    for c in (
        0.0034082910107109506,
        0.050955695062380861,
        0.18520832239976145,
        1.128379143519084,
    ):
        top = top * square + c
    low = jnp.full_like(at, -1.1791602954361697e-7)
    for c in (
        0.000023547966471313185,
        0.0010179625278914885,
        0.014070470171167667,
        0.11098505178285362,
        0.49746925110067538,
        1.0,
    ):
        low = low * square + c
    return at * top / low


def project_kernel(
    tokens, vectors, weight, normed_t, query_t, key, key_t, value, value_t
):
    norm, _ = normalize(tokens[...].astype(FULL))
    normed = (norm * vectors[0:1, :] + vectors[1:2, :]).astype(LOW)
    normed_t[...] = normed.T
    normed_t.done()
    half = key.shape[1]
    bias = vectors[6:8, :half]
    query_t[...] = ((dot(normed, weight[0], 1, 0) + bias[0:1]).astype(LOW) * score_scale).T
    query_t.done()
    held = dot(normed, weight[1], 1, 0).astype(LOW)
    key[...] = held
    key_t[...] = held.T
    key.done()
    key_t.done()
    held = (dot(normed, weight[2], 1, 0) + bias[1:2]).astype(LOW)
    value[...] = held
    value_t[...] = held.T


def attend_kernel(count, query_t, key, value_t, out_weight, attended_t, branch, *weights_t):
    keys, rows = key.shape[0], query_t.shape[1]
    heads = query_t.shape[0] // HEAD_DIM
    valid = lax.broadcasted_iota(jnp.int32, (keys, rows), 0) < count[0]
    for head in range(heads):
        pair = head // 2 * PAIR
        mine = lax.broadcasted_iota(jnp.int32, (PAIR, rows), 0) // HEAD_DIM == head % 2
        query = jnp.where(mine, query_t[pair : pair + PAIR, :], jnp.zeros((), LOW))
        scores = dot(key[:, pair : pair + PAIR], query, 1, 0)
        scores = jnp.where(valid, scores, MASKED)
        expo = jnp.exp(scores - jnp.max(scores, axis=0, keepdims=True))
        total = jnp.sum(expo, axis=0, keepdims=True)
        weights = (expo * (1.0 / total)).astype(LOW)
        weights_t[head][...] = weights
        weights_t[head].done()
        span = slice(head * HEAD_DIM, (head + 1) * HEAD_DIM)
        attended_t[span, :] = dot(value_t[span, :], weights, 1, 0).astype(LOW)
    branch[...] = dot(attended_t[...].T, out_weight[...], 1, 0)


def join_kernel(at, *refs):
    rows = refs[0].shape[0]
    for k, held in enumerate(refs[:RING]):
        owner = lax.rem(at[0] - k + RING, RING)
        refs[RING][pl.ds(pl.multiple_of(owner * rows, 8), rows), :] = held[...]


def clear_kernel(out):
    out[...] = jnp.zeros(out.shape, FULL)


def fold_kernel(blocks, out):
    total = blocks[0]
    for at in range(1, RING):
        total = total + blocks[at]
    out[...] = total


def add_kernel(held, arrived, out):
    out[...] = held[...] + arrived[...]


def quarter_kernel(at, *refs):
    summed, outs = refs[:-RING], refs[-RING:]
    rows = outs[0].shape[0]
    for k in (1, 2, 3, 0):
        owner = lax.rem(at[0] + k, RING)
        span = pl.ds(pl.multiple_of(owner * rows, 8), rows)
        total = summed[0][span, :]
        for held in summed[1:]:
            total = total + held[span, :]
        outs[k][...] = total


def piece_kernel(at, *refs):
    summed, (out, shared) = refs[:-2], refs[-2:]
    total = summed[0][...]
    for held in summed[1:]:
        total = total + held[...]
    out[...] = total
    shared[...] = total[at : at + 8]


def share_kernel(at, holds, mine, arrived, across, both, out):
    out[...] = mine[...] + arrived[...]
    rows = lax.broadcasted_iota(jnp.int32, across.shape, 0)
    extra = jnp.where((rows < 2) & (holds[0] == 1), across[...] + both[...], 0.0)
    out[at : at + 8, :] = out[at : at + 8, :] + extra


def hidden_kernel(
    start,
    count,
    tokens,
    own,
    other,
    vectors,
    up_bias,
    cotangent,
    *refs,
):
    tiles = up_bias.shape[1] // TILE
    up_weights, down_weights, refs = refs[:tiles], refs[tiles : 2 * tiles], refs[2 * tiles :]
    hidden_part(
        start, count, tokens, own, other, vectors, up_bias, cotangent, up_weights, down_weights, *refs
    )


def hidden_part(
    start,
    count,
    tokens,
    own,
    other,
    vectors,
    up_bias,
    cotangent,
    up_weights,
    down_weights,
    middle,
    normed,
    activated,
    grad_up,
    grad_down,
    grad_normed,
    up_sum,
    down_sum,
    *downward,
):
    rows, width = middle.shape
    held = tokens[...].astype(FULL) + (own[...] + other[...]) + vectors[4:5, :]
    middle[...] = held
    middle.done()
    norm, _ = normalize(held)
    normed_low = (norm * vectors[2:3, :] + vectors[3:4, :]).astype(LOW)
    normed[...] = normed_low
    normed.done()
    valid = lax.broadcasted_iota(jnp.int32, (rows, 1), 0) + start < count[0]
    grad_out = jnp.where(valid, cotangent[...].astype(FULL), 0.0)
    down_sum[...] = jnp.sum(grad_out, axis=0, keepdims=True)
    grad_low = grad_out.astype(LOW)
    grad_down[...] = grad_low
    grad_down.done()
    for tile, (up_weight, down_weight) in enumerate(zip(up_weights, down_weights)):
        at = tile * TILE
        span = slice(at, at + TILE)
        upward = dot(normed_low, up_weight[...], 1, 0) + up_bias[0:1, span]
        share = 0.5 + 0.5 * erf(upward * root_half)
        active = (upward * share).astype(LOW)
        activated[:, span] = active
        slope = share + upward * (root_two_pi * jnp.exp(-0.5 * upward * upward))
        pushed = (dot(grad_low, down_weight[...], 1, 1) * slope).astype(LOW)
        grad_up[:, span] = pushed
        up_sum[:, span] = jnp.sum(pushed.astype(FULL), axis=0, keepdims=True)
        back = dot(pushed, up_weight[...], 1, 1)
        ahead = dot(active, down_weight[...], 1, 0)
        if at == 0:
            grad_normed[...] = back
            total = ahead
        else:
            grad_normed[...] = grad_normed[...] + back
            total = total + ahead
    for at, share in enumerate(downward):
        share[...] = total[at * SHARE : (at + 1) * SHARE]


def attend_back(refs, put):
    (
        grad_down,
        middle,
        own,
        other,
        vectors,
        out_weight,
        query_t,
        key_t,
        value,
        *weights_t,
        grad_branch,
        grad_middle,
        sums,
    ) = refs
    heads = len(weights_t)
    rows = middle.shape[0]
    norm, scale = normalize(middle[...])
    grad = own[...] + other[...]
    sums[0:1, :] = jnp.sum(grad * norm, axis=0, keepdims=True)
    sums[1:2, :] = jnp.sum(grad, axis=0, keepdims=True)
    held = grad_down[...].astype(FULL) + norm_back(grad, vectors[2:3, :], norm, scale)
    grad_middle[...] = held
    grad_middle.done()
    sums[2:3, :] = jnp.sum(held, axis=0, keepdims=True)
    branch = held.astype(LOW)
    grad_branch[...] = branch
    grad_branch.done()
    grad_att = dot(out_weight[...], branch, 1, 1).astype(LOW)
    for head in range(heads):
        pair = head // 2 * PAIR
        span = slice(head * HEAD_DIM, (head + 1) * HEAD_DIM)
        mine = lax.broadcasted_iota(jnp.int32, (PAIR, rows), 0) // HEAD_DIM == head % 2
        grad_own = jnp.where(mine, grad_att[pair : pair + PAIR, :], jnp.zeros((), LOW))
        grad_probs = dot(value[:, pair : pair + PAIR], grad_own, 1, 0)
        weights = weights_t[head][...]
        probs = weights.astype(FULL)
        shift = jnp.sum(grad_probs * probs, axis=0, keepdims=True)
        grad_scores = (probs * (grad_probs - shift)).astype(LOW)
        put(
            span,
            dot(key_t[span, :], grad_scores, 1, 0) * score_scale,
            dot(query_t[span, :], grad_scores, 1, 1),
            dot(grad_att[span, :], weights, 1, 1),
        )


def attend_back_kernel(*refs):
    *refs, grad_query_t, grad_key_t, grad_value_t = refs

    def put(span, query, key, value):
        grad_query_t[span, :] = query
        grad_key_t[span, :] = key
        grad_value_t[span, :] = value

    attend_back(refs, put)


def attend_last_kernel(heads, *refs):
    refs, (queries, keys, values) = refs[:-3], refs[-3:]
    inputs, refs = refs[: 9 + heads], refs[9 + heads :]
    before = [refs[i * (SPLIT - 1) : (i + 1) * (SPLIT - 1)] for i in range(3)]
    refs = refs[3 * (SPLIT - 1) :]
    tokens, weight, grad_branch, grad_middle, back_sums, query, key, value, sums, *shares = refs

    def put(span, grad_query, grad_key, grad_value):
        queries[span, :] = grad_query
        keys[span, :] = sum((k[span, :] for k in before[1]), grad_key)
        values[span, :] = sum((v[span, :] for v in before[2]), grad_value)

    attend_back([*inputs, grad_branch, grad_middle, back_sums], put)
    pieces = [
        jnp.concatenate([q[...] for q in before[0]] + [queries[...]], axis=1),
        keys[...],
        values[...],
    ]
    total = None
    for at, (piece, out) in enumerate(zip(pieces, (query, key, value))):
        low = piece.T.astype(LOW)
        out[...] = low
        out.done()
        if at != 1:
            sums[0:1, (at // 2) * low.shape[1] : (at // 2 + 1) * low.shape[1]] = jnp.sum(
                low.astype(FULL), axis=0, keepdims=True
            )
        term = dot(low, weight[at], 1, 1)
        total = term if total is None else total + term
    for at, share in enumerate(shares):
        share[...] = total[at * SHARE : (at + 1) * SHARE]
        share.done()
    norm, _ = normalize(tokens[...].astype(FULL))
    sums[1:2, :] = jnp.sum(total * norm, axis=0, keepdims=True)
    sums[2:3, :] = jnp.sum(total, axis=0, keepdims=True)


def hidden_grads(owner, refs, put):
    activated, grad_down, normed, grad_up = (refs[i * SPLIT : (i + 1) * SPLIT] for i in range(4))
    tall, short = activated[0].shape[1] // 2, normed[0].shape[1] // 2
    width = grad_down[0].shape[1]
    columns = pl.ds(pl.multiple_of(owner * tall, PAIR), tall)
    active = [a[:, columns].T for a in activated]
    columns = pl.ds(pl.multiple_of(owner * short, PAIR), short)
    inner = [n[:, columns].T for n in normed]
    down_rows, up_rows = tall // 16, short // 16
    rows = down_rows + 2 * up_rows

    def product(lefts, rights, span):
        total = dot(lefts[0][span], rights[0][...], 1, 0)
        for left, right in zip(lefts[1:], rights[1:]):
            total = total + dot(left[span], right[...], 1, 0)
        return total

    for x in range(RING):
        down = product(active, grad_down, slice(x * RING * down_rows, (x + 1) * RING * down_rows))
        up = product(inner, grad_up, slice(x * RING * up_rows, (x + 1) * RING * up_rows))
        for y in range(RING):
            at = pl.multiple_of(jnp.where(owner == 0, x * RING + y, y * RING + x) * rows, 8)
            put(at, down[y * down_rows : (y + 1) * down_rows])
            part = up[y * up_rows : (y + 1) * up_rows]
            put(at + down_rows, part[:, :width])
            put(at + down_rows + up_rows, part[:, width:])


def hidden_away_kernel(away, *refs):
    *refs, lower, upper = refs
    half = lower.shape[0]

    def put(at, value):
        rows = value.shape[0]
        here = pl.ds(pl.multiple_of(jnp.where(at < half, at, at - half), 8), rows)

        @pl.when(at < half)
        def _():
            lower[here, :] = value

        @pl.when(at >= half)
        def _():
            upper[here, :] = value

    hidden_grads(away[0], refs, put)


def hidden_home_kernel(side, *refs):
    *refs, lower, upper, out = refs
    half = lower.shape[0]

    def put(at, value):
        out[pl.ds(pl.multiple_of(at, 8), value.shape[0]), :] = value

    hidden_grads(side[0], refs, put)
    out[:half, :] = out[:half, :] + lower[...]
    out[half:, :] = out[half:, :] + upper[...]


def spread_kernel(gathered, down_out, up_out):
    members, rows, width = gathered.shape
    tall, short = rows // 2, rows // 4
    for at in range(members):
        down_out[at * tall : (at + 1) * tall, :] = gathered[at, :tall, :]
        span = slice(at * short, (at + 1) * short)
        up_out[span, :width] = gathered[at, tall : tall + short, :]
        up_out[span, width:] = gathered[at, tall + short :, :]


def late_grads(at, refs):
    grads, refs = refs[:3], refs[3:]
    attended, branch, back, up_sum, down_sum = (refs[i * SPLIT : (i + 1) * SPLIT] for i in range(5))
    normed_t, sums, out = refs[5 * SPLIT :]
    local, width = attended[0].shape[0], normed_t.shape[0]
    short = width // 2
    mine = pl.ds(pl.multiple_of(at * short, PAIR), short)
    for part, grad in enumerate(grads):
        out[part * short : (part + 1) * short, :] = dot(normed_t[mine, :], grad[...], 1, 0)
    total = dot(attended[0][...].astype(LOW), branch[0][:, mine], 1, 0)
    for a, b in zip(attended[1:], branch[1:]):
        total = total + dot(a[...].astype(LOW), b[:, mine], 1, 0)
    out[3 * short : 3 * short + local, :] = total
    end = 3 * short + local
    out[end:, :] = jnp.zeros((out.shape[0] - end, out.shape[1]), FULL)
    out[end : end + 1, :] = sums[1:2, mine]
    out[end + 1 : end + 2, :] = sums[2:3, mine]
    out[end + 2 : end + 3, :] = sums[0:1, mine]
    for row, of in ((3, 2), (4, 0), (5, 1)):
        out[end + row : end + row + 1, :] = sum(
            (b[of : of + 1, mine] for b in back[1:]), back[0][of : of + 1, mine]
        )
    for part in range(2):
        inner = pl.ds(pl.multiple_of(part * width + at * short, PAIR), short)
        out[end + 6 + part : end + 7 + part, :] = sum(
            (u[:, inner] for u in up_sum[1:]), up_sum[0][:, inner]
        )
    out[end + 8 : end + 9, :] = sum((d[:, mine] for d in down_sum[1:]), down_sum[0][:, mine])
    out.done()


def late_grads_kernel(side, *refs):
    *refs, away, home = refs
    late_grads(1 - side[0], [*refs, away])
    late_grads(side[0], [*refs, home])


def unpack_kernel(side, mine, other, qkv_grad, out_grad, vectors):
    short = out_grad.shape[1] // 2
    local = out_grad.shape[0]
    end = 3 * short + local
    for owner, held in ((side[0], mine), (1 - side[0], other)):
        span = pl.ds(pl.multiple_of(owner * short, PAIR), short)
        for part in range(3):
            qkv_grad[part, span, :] = held[part * short : (part + 1) * short, :]
        out_grad[:, span] = held[3 * short : end, :]
        vectors[:, span] = held[end : end + vectors.shape[0], :]


def finish_kernel(count, tokens, vectors, *refs):
    grad_middle, middle, refs = refs[:SPLIT], refs[SPLIT : 2 * SPLIT], refs[2 * SPLIT :]
    tokens_grad, block_out = refs[-2:]
    count_shares = tokens.shape[0] // SHARE
    each = count_shares // SPLIT
    own, other = refs[: 2 * count_shares], refs[2 * count_shares : -2]
    for at in range(count_shares):
        span = slice(at * SHARE, (at + 1) * SHARE)
        inner = slice(at % each * SHARE, (at % each + 1) * SHARE)
        valid = lax.broadcasted_iota(jnp.int32, (SHARE, 1), 0) + at * SHARE < count[0]
        total = middle[at // each][inner, :] + (own[at][...] + other[at][...]) + vectors[5:6, :]
        block_out[span, :] = jnp.where(valid, total, 0.0).astype(LOW)
    block_out.done()
    for at in range(count_shares):
        span = slice(at * SHARE, (at + 1) * SHARE)
        inner = slice(at % each * SHARE, (at % each + 1) * SHARE)
        norm, scale = normalize(tokens[span, :].astype(FULL))
        grad = own[count_shares + at][...] + other[count_shares + at][...]
        tokens_grad[span, :] = (
            grad_middle[at // each][inner, :] + norm_back(grad, vectors[0:1, :], norm, scale)
        ).astype(LOW)


def far(array):
    return pltpu.with_memory_space_constraint(array, pltpu.HBM)


class Arriving:
    def __init__(self, move, held):
        self.move, self.held = move, held
        self.shape, self.dtype = held.shape, held.dtype

    def __getitem__(self, at):
        if self.move is not None:
            self.move.wait()
            self.move = None
        return self.held[at]


class Leaving:
    def __init__(self, made, result, semaphore):
        self.made, self.result, self.semaphore = made, result, semaphore
        self.shape, self.dtype = made.shape, made.dtype
        self.move = None

    def __getitem__(self, at):
        return self.made[at]

    def __setitem__(self, at, value):
        self.made[at] = value

    def done(self):
        if self.move is None:
            self.move = pltpu.make_async_copy(self.made, self.result, self.semaphore)
            self.move.start()


class Line:
    def __init__(self):
        self.last = []
        self.far = False
        self.moves = Moves()

    def pause(self):
        self.call(clear_kernel, [((8, PAIR), FULL)], long=True, near=True, name="pause")

    def call(
        self,
        kernel,
        outs,
        *args,
        scalars=0,
        blocks=None,
        waits=(),
        long=False,
        near=False,
        scratch=(),
        name=None,
    ):
        waits = [*self.last, *waits]
        spaces = [pltpu.HBM if self.far else pl.ANY] * len(self.last)
        spaces += [pl.ANY] * (len(waits) - len(self.last))
        waits = [far(w) if space == pltpu.HBM else w for w, space in zip(waits, spaces)]
        wait_specs = [pl.BlockSpec(memory_space=space) for space in spaces]
        count, arrays = len(args), args[scalars:]
        seen = [
            (blocks or {}).get(number, (a.shape, (0,) * a.ndim))
            for number, a in enumerate(arrays, scalars)
        ]
        options = dict(
            compiler_params=pltpu.CompilerParams(vmem_limit_bytes=(20 if near else 48) << 20),
            cost_estimate=pl.CostEstimate(
                flops=10**11 if long else 0, bytes_accessed=0, transcendentals=0
            ),
            name=name,
        )
        specs = [pl.BlockSpec(memory_space=pltpu.SMEM)] * scalars
        if near:
            results = pl.pallas_call(
                lambda *refs: kernel(*refs[:count], *refs[count + len(waits) :]),
                grid=(1,),
                out_shape=[jax.ShapeDtypeStruct(*out) for out in outs],
                in_specs=specs
                + [pl.BlockSpec(shape, lambda _, at=at: at) for shape, at in seen]
                + wait_specs,
                out_specs=[
                    pl.BlockSpec(shape, lambda _, n=len(shape): (0,) * n) for shape, _ in outs
                ],
                **options,
            )(*args, *waits)
            self.last, self.far = [min(results, key=lambda r: r.size)], False
            return list(results)

        moved = [any(a is m for m in self.moves) for a in arrays]

        def run(*refs):
            given, refs = refs[:count], refs[count + len(waits) :]
            results, refs = refs[: len(outs)], refs[len(outs) :]
            held, refs = refs[: len(arrays)], refs[len(arrays) :]
            made, refs = refs[: len(outs)], refs[len(outs) :]
            arrive, leave, *own = refs
            arriving = []
            for at, (array, (shape, spot), into) in enumerate(zip(given[scalars:], seen, held)):
                if shape != array.shape:
                    array = array.at[tuple(pl.ds(i * n, n) for i, n in zip(spot, shape))]
                move = pltpu.make_async_copy(array, into, arrive.at[at])
                move.start()
                arriving.append(Arriving(move, into))
            leaving = [
                Leaving(source, result, leave.at[at])
                for at, (source, result) in enumerate(zip(made, results))
            ]
            kernel(*given[:scalars], *arriving, *leaving, *own)
            for held in arriving:
                if held.move is not None:
                    held.move.wait()
            for out in leaving:
                out.done()
            for out in leaving:
                out.move.wait()

        results = pl.pallas_call(
            run,
            out_shape=[pltpu.HBM(*out) for out in outs],
            in_specs=specs
            + [pl.BlockSpec(memory_space=pl.ANY if m else pltpu.HBM) for m in moved]
            + wait_specs,
            out_specs=[pl.BlockSpec(memory_space=pltpu.HBM)] * len(outs),
            scratch_shapes=[pltpu.VMEM(shape, a.dtype) for a, (shape, _) in zip(arrays, seen)]
            + [pltpu.VMEM(*out) for out in outs]
            + [pltpu.SemaphoreType.DMA((len(arrays),)), pltpu.SemaphoreType.DMA((len(outs),))]
            + [pltpu.VMEM(*own) for own in scratch],
            **options,
        )(*args[:scalars], *(a if m else far(a) for a, m in zip(arrays, moved)), *waits)
        self.last, self.far = [min(results, key=lambda r: r.size)], True
        return list(results)


def body(
    tokens,
    counts,
    ln1_gain,
    ln1_bias,
    qkv_weight,
    qv_bias,
    out_weight,
    out_bias,
    ln2_gain,
    ln2_bias,
    up_weight,
    up_bias,
    down_weight,
    down_bias,
    cotangent,
):
    items, patches, width = tokens.shape
    local = qkv_weight.shape[2]
    heads = local // HEAD_DIM
    hidden = up_weight.shape[1]
    part = patches // SPLIT
    spot = core, x, y = places()
    side, away = core.reshape(1), (1 - core).reshape(1)
    first, second = jnp.where(core == 0, x, y), jnp.where(core == 0, y, x)
    line = Line()
    moves = line.moves
    tokens = tokens.reshape(patches, width)
    cotangent = cotangent.reshape(patches, width)
    weight = qkv_weight.transpose(1, 0, 2)
    starts = [part * i for i in range(SPLIT)]

    at_row = lax.broadcasted_iota(jnp.int32, (8, width), 0)
    vectors = jnp.zeros((8, width), LOW)
    for row, vector in enumerate((ln1_gain, ln1_bias, ln2_gain, ln2_bias, out_bias, down_bias)):
        vectors = jnp.where(at_row == row, vector[None, :], vectors)
    for row in range(2):
        both = jnp.concatenate([qv_bias[row], qv_bias[row]])
        vectors = jnp.where(at_row == 6 + row, both[None, :], vectors)
    vectors = vectors.astype(FULL)
    up_bias = jnp.broadcast_to(up_bias.astype(FULL)[None, :], (8, hidden))

    normed_t, query_t, key, key_t, value, value_t = line.call(
        project_kernel,
        [((width, patches), LOW)]
        + [((local, patches), LOW), ((patches, local), LOW)]
        + [((local, patches), LOW), ((patches, local), LOW), ((local, patches), LOW)],
        tokens,
        vectors,
        weight,
        name="project",
    )

    def attend(at):
        attended, branch, *weights = line.call(
            attend_kernel,
            [((local, part), LOW), ((part, width), FULL)] + [((patches, part), LOW)] * heads,
            counts,
            query_t,
            key,
            value_t,
            out_weight,
            scalars=1,
            blocks={1: ((local, part), (0, at))},
            name="attend",
        )
        return attended, branch, weights

    attended, branches, weights = zip(*[attend(at) for at in range(SPLIT)])
    others = [moves.over_tensor(b) for b in branches]

    tiles = hidden // TILE

    def feed_forward(at):
        block = ((part, width), (at, 0))
        return line.call(
            partial(hidden_kernel, starts[at]),
            [
                ((part, width), FULL),
                ((part, width), LOW),
                ((part, hidden), LOW),
                ((part, hidden), LOW),
                ((part, width), LOW),
                ((part, width), FULL),
                ((1, hidden), FULL),
                ((1, width), FULL),
            ]
            + [((SHARE, width), FULL)] * (part // SHARE),
            counts,
            tokens,
            branches[at],
            others[at],
            vectors,
            up_bias,
            cotangent,
            *[up_weight] * tiles,
            *[down_weight] * tiles,
            scalars=1,
            blocks={1: block, 6: block}
            | {7 + t: ((width, TILE), (0, t)) for t in range(tiles)}
            | {7 + tiles + t: ((TILE, width), (t, 0)) for t in range(tiles)},
            name="hidden",
        )

    (
        middle,
        normed_two,
        activated,
        grad_up,
        grad_down,
        grad_normed_two,
        up_sum,
        down_sum,
        *downward,
    ) = zip(*[feed_forward(at) for at in range(SPLIT)])
    grad_others = [moves.over_tensor(g) for g in grad_normed_two]

    grads_in = [*activated, *grad_down, *normed_two, *grad_up]
    block_rows = hidden // 32 + width // 16
    hidden_away = line.call(
        hidden_away_kernel,
        [((8 * block_rows, width), FULL)] * 2,
        away,
        *grads_in,
        scalars=1,
        name="hidden_away",
    )
    hidden_arrived = [moves.over_cores(a) for a in hidden_away]

    def back_in(at):
        return [
            grad_down[at],
            middle[at],
            grad_normed_two[at],
            grad_others[at],
            vectors,
            out_weight,
            query_t,
            key_t,
            value,
            *weights[at],
        ]

    back_out = [((part, width), LOW), ((part, width), FULL), ((8, width), FULL)]
    back_held = [((local, part), FULL), ((local, patches), FULL), ((local, patches), FULL)]
    back_parts = [
        line.call(
            attend_back_kernel,
            back_out + back_held,
            *back_in(at),
            blocks={6: ((local, part), (0, at))},
            long=True,
            name="attend_back",
        )
        for at in range(SPLIT - 1)
    ]
    hidden_mine = line.call(
        hidden_home_kernel,
        [((16 * block_rows, width), FULL)],
        side,
        *grads_in,
        *hidden_arrived,
        scalars=1,
        name="hidden_home",
    )[0]
    hidden_mine = moves.exchange(hidden_mine.reshape(RING, 4 * block_rows, width), rings(True))
    grad_branch, grad_middle, back_sums, grad_query, grad_key, grad_value = zip(*back_parts)
    branch_last, middle_last, sums_last, grad_query, grad_key, grad_value, late, *shares = line.call(
        partial(attend_last_kernel, heads),
        back_out
        + [((patches, local), LOW)] * 3
        + [((8, width), FULL)]
        + [((SHARE, width), FULL)] * (patches // SHARE),
        *back_in(SPLIT - 1),
        *grad_query,
        *grad_key,
        *grad_value,
        tokens,
        weight,
        blocks={6: ((local, part), (0, SPLIT - 1))},
        scratch=back_held,
        long=True,
        name="attend_last",
    )
    grad_branch += (branch_last,)
    grad_middle += (middle_last,)
    back_sums += (sums_last,)
    late_rows = 3 * width // 2 + local + 128

    shares = [*(d[at] for at in range(SPLIT) for d in downward), *shares]
    other_shares = [moves.over_tensor(s) for s in shares]
    late_away, late_home = line.call(
        late_grads_kernel,
        [((late_rows, local), FULL)] * 2,
        side,
        grad_query,
        grad_key,
        grad_value,
        *attended,
        *grad_branch,
        *back_sums,
        *up_sum,
        *down_sum,
        normed_t,
        late,
        scalars=1,
        name="late_grads",
    )
    late_arrived = moves.over_cores(late_away)

    def fold(blocks, *waits, near=False):
        return line.call(
            fold_kernel,
            [(blocks.shape[1:], FULL)],
            blocks,
            waits=waits,
            near=near,
            name="hidden_sums",
        )[0]

    def quarter(summed, at, *waits, near=True):
        rows = summed[0].shape[0] // RING
        return line.call(
            quarter_kernel,
            [((rows, local), FULL)] * RING,
            at.reshape(1),
            *summed,
            scalars=1,
            waits=waits,
            near=near,
            name="late_sums",
        )

    def join(block, arrived, at, *waits):
        return line.call(
            join_kernel,
            [((RING * block.shape[0], local), FULL)],
            at.reshape(1),
            block,
            *arrived,
            scalars=1,
            waits=waits,
            near=True,
            name="late_join",
        )[0]

    hidden_mine = fold(hidden_mine)
    hidden_mine = moves.exchange(hidden_mine.reshape(RING, block_rows, width), rings(False))
    mine, *sent = quarter([late_home, late_arrived], first, near=False)
    late_sums = [mine, *moves.around(sent, first_shift)]
    line.pause()
    hidden_mine = fold(hidden_mine, near=True)
    hidden_arrived = moves.to(hidden_mine, "dp", Z_SWAP)
    mine, *sent = quarter(late_sums, second, *other_shares[:4])
    late_sums = [mine, *moves.around(sent, second_shift)]
    hidden_mine = line.call(
        add_kernel,
        [(hidden_mine.shape, FULL)],
        hidden_mine,
        hidden_arrived,
        near=True,
        name="hidden_sums",
    )[0]
    hidden_all = lax.all_gather(
        hidden_mine, "dp", axis_index_groups=PLANES, axis=0, tiled=False
    )
    norm_block, norm_at = divmod(3 * width // 2 + local, late_rows // 16)
    mine, shared = line.call(
        partial(piece_kernel, norm_at),
        [(mine.shape, FULL), ((8, local), FULL)],
        *late_sums,
        waits=[other_shares[4]],
        near=True,
        name="late_piece",
    )
    arrived = [
        moves.to(mine, "dp", Z_SWAP),
        moves.over_tensor(shared),
        moves.to(shared, ("dp", "tensor"), BOTH_SWAP),
    ]
    mine = line.call(
        partial(share_kernel, norm_at),
        [(mine.shape, FULL)],
        (first * RING + second == norm_block).astype(jnp.int32).reshape(1),
        mine,
        *arrived,
        scalars=1,
        near=True,
        name="late_share",
    )[0]
    arrived = moves.around([mine] * (RING - 1), second_shift)
    mine = join(mine, arrived, second, other_shares[5])
    arrived = moves.around([mine] * (RING - 1), first_shift)
    tokens_grad, block_out = line.call(
        finish_kernel,
        [((patches, width), LOW)] * 2,
        counts,
        tokens,
        vectors,
        *grad_middle,
        *middle,
        *shares,
        *other_shares,
        scalars=1,
        name="finish",
    )
    mine = join(mine, arrived, first)
    other = moves.over_cores(mine)
    each = 8
    members = 32 // each
    down_weight_grad, up_weight_grad = pl.pallas_call(
        lambda gathered, _, *outs: spread_kernel(gathered, *outs),
        grid=(each,),
        out_shape=[
            jax.ShapeDtypeStruct((hidden, width), FULL),
            jax.ShapeDtypeStruct((width, hidden), FULL),
        ],
        in_specs=[
            pl.BlockSpec((members, *hidden_all.shape[1:]), lambda i: (i, 0, 0)),
            pl.BlockSpec(memory_space=pl.ANY),
        ],
        out_specs=[
            pl.BlockSpec((hidden // each, width), lambda i: (i, 0)),
            pl.BlockSpec((width // each, hidden), lambda i: (i, 0)),
        ],
        compiler_params=pltpu.CompilerParams(vmem_limit_bytes=48 << 20),
        name="spread",
    )(hidden_all, *line.last)
    line.last, line.far = [down_weight_grad], False
    qkv_weight_grad, out_weight_grad, small = line.call(
        unpack_kernel,
        [((3, width, local), FULL), ((local, width), FULL), ((9, width), FULL)],
        side,
        mine,
        other,
        scalars=1,
        name="unpack",
    )
    qkv_weight_grad = qkv_weight_grad.transpose(1, 0, 2)
    ln1_gain_grad, ln1_bias_grad, qv_bias_grad, out_bias_grad, ln2_gain_grad, ln2_bias_grad = (
        small[i] for i in range(6)
    )
    up_bias_grad = small[6:8].reshape(hidden)
    down_bias_grad = small[8]
    return (
        block_out.reshape(items, patches, width),
        tokens_grad.reshape(items, patches, width),
        ln1_gain_grad,
        ln1_bias_grad,
        qkv_weight_grad,
        qv_bias_grad.reshape(2, local),
        out_weight_grad,
        out_bias_grad,
        ln2_gain_grad,
        ln2_bias_grad,
        up_weight_grad,
        up_bias_grad,
        down_weight_grad,
        down_bias_grad,
    )


def solution(mesh):
    in_specs = (
        P("dp", None, None),
        P("dp"),
        P(),
        P(),
        P(None, None, "tensor"),
        P(None, "tensor"),
        P("tensor", None),
        P(),
        P(),
        P(),
        P(None, "tensor"),
        P("tensor"),
        P("tensor", None),
        P(),
        P("dp", None, None),
    )
    out_specs = (
        P("dp", None, None),
        P("dp", None, None),
        P(),
        P(),
        P(None, None, "tensor"),
        P(None, "tensor"),
        P("tensor", None),
        P(),
        P(),
        P(),
        P(None, "tensor"),
        P("tensor"),
        P("tensor", None),
        P(),
    )
    return jax.shard_map(body, mesh=mesh, in_specs=in_specs, out_specs=out_specs, check_vma=False)
```
